512 devices in a mesh: blk: 128 (over z, x_hi, y), feat: 4 (over x_lo, core).
Axes of the slice: x: 4 (x_hi: 2, x_lo: 2; x = x_hi * 2 + x_lo), y: 4, z: 16, core: 2. Of those that a mesh axis runs over, the one named last changes fastest.
Arguments:
- layer_inputs: bfloat16 [1024, 2304], P('blk', 'feat'), may hold values from -6 to 6
- mlp_targets: bfloat16 [1024, 2304], P('blk', 'feat'), may hold values from -6 to 6
- enc_weight: bfloat16 [65536, 2304], P('blk', 'feat'), may hold values from -0.125 to 0.125
- enc_bias: float32 [65536], P('blk'), may hold values from -3 to 3
- act_mask: int32 [65536, 256], P('blk'), may hold values 0 or 1
- dec_weight: bfloat16 [163840, 2304], P('blk', 'feat'), may hold values from -0.046875 to 0.046875
- owner_half: int32 [128], P('blk'), may hold values from 0 to 1, as said below
Outputs:
- reconstruction: bfloat16 [1024, 2304], P('blk', 'feat')
- enc_grad: bfloat16 [65536, 2304], P('blk', 'feat')
- bias_grad: float32 [65536], P('blk')
- dec_grad: bfloat16 [163840, 2304], P('blk', 'feat')
The draws below stay inside these ranges and needn't reach their ends.
Inputs may be any that keep to these rules, and one draw needn't show every extreme that they name: owner_half[s * 32 + g] + owner_half[(3 - s) * 32 + g] = 1 for every layer s and position g.
All inputs are finite; a program needn't handle non-finite values. No bound on the sum of `act_mask` on one device may be relied on, other than what follows from the above.
Results may differ from the reference program's by a relative error of at most 0.012.
Values may be sent and summed in bfloat16 or wider, within the bound.
No kernel may reach another device: no remote copies, remote signals or barrier semaphores. Data moves between devices by JAX's collectives and lax.ppermute only.
A program may use at most 64 MiB of HBM per device.

```python
import jax
import jax.numpy as jnp
from jax import lax

D = 2304
F = 16384
LAYERS = 4
TOKENS = 256
GROUP = 32
SPAN = 256
SLOTS = 5


def draw_owner_half(key, part):
    key = jax.random.fold_in(key, 7)
    lower = jax.random.randint(key, (LAYERS // 2, GROUP), 0, 2)
    full_table = jnp.concatenate([lower, (1 - lower)[::-1]], axis=0)
    return full_table.reshape(LAYERS * GROUP).astype(jnp.int32)


def touch_ends(entries, key, low, top_value):
    longest = entries.shape.index(max(entries.shape))
    spots = []
    for shift in (0, 1):
        where = [jax.random.randint(jax.random.fold_in(key, axis), (), 0, length) for axis, length in enumerate(entries.shape)]
        where[longest] = (where[longest] + shift) % entries.shape[longest]
        spots.append(tuple(where))
    return entries.at[spots[0]].set(low).at[spots[1]].set(top_value)


def shard_levels(stream_key, dims, split, low, largest):
    loudness, own = 1.0, jax.random.fold_in(stream_key, 6)
    for position, shards_of in split:
        heights = jnp.exp(jax.random.uniform(jax.random.fold_in(own, position), (shards_of,), jnp.float32, low / len(split), largest / len(split)))
        loudness = loudness * jnp.repeat(heights, dims[position] // shards_of).reshape([-1 if axis == position else 1 for axis in range(len(dims))])
    return loudness


def bell_draw(rng, shape, spread, bound, shards=(), held_as=jnp.bfloat16):
    loudness = shard_levels(rng, shape, shards, -0.22, 0.18) if shards else 1.0
    array = jax.random.normal(rng, shape, jnp.float32) * spread * loudness
    return jnp.minimum(jnp.maximum(array, -bound), bound).astype(held_as)


def setup_inputs(seed: int = 0) -> dict:
    splits = jax.random.split(jax.random.key(seed), 8)
    return {
        "layer_inputs": bell_draw(splits[0], (LAYERS * TOKENS, D), 1.0, 6.0, ((0, 128), (1, 4))),
        "mlp_targets": bell_draw(splits[1], (LAYERS * TOKENS, D), 1.0, 6.0, ((0, 128), (1, 4))),
        "enc_weight": bell_draw(splits[2], (LAYERS * F, D), D ** -0.5, 0.125, ((0, 128), (1, 4))),
        "enc_bias": bell_draw(splits[3], (LAYERS * F,), 0.5, 3.0, ((0, 128),), jnp.float32),
        "act_mask": touch_ends((jax.random.randint(splits[4], (LAYERS * F, TOKENS), 0, 2) < 1).astype(jnp.int32), jax.random.fold_in(splits[4], 1), 0, 1),
        "dec_weight": bell_draw(splits[5], (LAYERS * GROUP * SLOTS * SPAN, D), F ** -0.5, 0.046875, ((0, 128), (1, 4))),
        "owner_half": draw_owner_half(jax.random.fold_in(splits[7], 71), 0),
    }


def build_plan():
    slot_plan = []
    for source in range(LAYERS):
        for slot_index in range(SLOTS):
            if slot_index < LAYERS - source:
                slot_plan.append((source, slot_index, source + slot_index, True))
            else:
                slot_plan.append((source, slot_index, slot_index - 1, False))
    return slot_plan


def reference(layer_inputs, mlp_targets, enc_weight, enc_bias, act_mask, dec_weight, owner_half):
    highest = lax.Precision.HIGHEST
    inputs_f = layer_inputs.reshape(LAYERS, TOKENS, D).astype(jnp.float32)
    weights_f = enc_weight.reshape(LAYERS, F, D).astype(jnp.float32)
    pre_acts = jnp.einsum("lfd,lmd->lfm", weights_f, inputs_f, precision=highest)
    pre_acts = pre_acts + enc_bias.reshape(LAYERS, F)[:, :, None]
    mask_values = act_mask.astype(jnp.float32).reshape(LAYERS, F, TOKENS)
    code_all = (mask_values * pre_acts).astype(jnp.bfloat16)
    code_all = lax.optimization_barrier(code_all)
    code_split = code_all.astype(jnp.float32).reshape(LAYERS, GROUP, 2, SPAN, TOKENS)
    side_table = owner_half.reshape(LAYERS, GROUP)[:, :, None, None]
    own_codes = jnp.where(side_table == 0, code_split[:, :, 0], code_split[:, :, 1])
    mirrored = code_split[::-1]
    other_codes = jnp.where(side_table == 0, mirrored[:, :, 0], mirrored[:, :, 1])
    decoder = dec_weight.reshape(LAYERS, GROUP, SLOTS, SPAN, D)
    slot_plan = build_plan()
    recon_list = [jnp.zeros((TOKENS, D), jnp.float32)] * LAYERS
    for source, slot_index, target, is_own in slot_plan:
        slot_codes = own_codes[source] if is_own else other_codes[source]
        slot_rows = decoder[source, :, slot_index].astype(jnp.float32)
        recon_list[target] = recon_list[target] + jnp.einsum("grm,grd->md", slot_codes, slot_rows, precision=highest)
    recon_all = jnp.stack(recon_list)
    targets_f = mlp_targets.reshape(LAYERS, TOKENS, D).astype(jnp.float32)
    error_grad = (recon_all - targets_f).astype(jnp.bfloat16)
    error_grad = lax.optimization_barrier(error_grad)
    error_f = error_grad.astype(jnp.float32)
    own_grads = [jnp.zeros((GROUP, SPAN, TOKENS), jnp.float32)] * LAYERS
    other_grads = [jnp.zeros((GROUP, SPAN, TOKENS), jnp.float32)] * LAYERS
    grads_by_source = [[] for source in range(LAYERS)]
    for source, slot_index, target, is_own in slot_plan:
        slot_codes = own_codes[source] if is_own else other_codes[source]
        slot_rows = decoder[source, :, slot_index].astype(jnp.float32)
        row_grad = jnp.einsum("grm,md->grd", slot_codes, error_f[target], precision=highest)
        grads_by_source[source].append(row_grad.astype(jnp.bfloat16))
        term = jnp.einsum("grd,md->grm", slot_rows, error_f[target], precision=highest)
        if is_own:
            own_grads[source] = own_grads[source] + term
        else:
            other_grads[source] = other_grads[source] + term
    dec_grad = jnp.stack([jnp.stack(items, axis=1) for items in grads_by_source])
    dec_grad = dec_grad.reshape(LAYERS * GROUP * SLOTS * SPAN, D)
    own_stack = jnp.stack(own_grads)
    other_by_layer = jnp.stack(other_grads)[::-1]
    first_half = jnp.where(side_table == 0, own_stack, other_by_layer)
    second_half = jnp.where(side_table == 0, other_by_layer, own_stack)
    code_grad = jnp.stack([first_half, second_half], axis=2).reshape(LAYERS, F, TOKENS)
    pre_grad = mask_values * code_grad
    bias_grad = jnp.sum(pre_grad, axis=2).reshape(LAYERS * F)
    pre_round = pre_grad.astype(jnp.bfloat16)
    pre_round = lax.optimization_barrier(pre_round)
    enc_grad = jnp.einsum("lfm,lmd->lfd", pre_round.astype(jnp.float32), inputs_f, precision=highest)
    enc_grad = enc_grad.astype(jnp.bfloat16).reshape(LAYERS * F, D)
    reconstruction = recon_all.astype(jnp.bfloat16).reshape(LAYERS * TOKENS, D)
    return (reconstruction, enc_grad, bias_grad, dec_grad)
```

```python
import jax
import jax.numpy as jnp
from jax import lax
from jax.sharding import Mesh, PartitionSpec as P

LAYERS = 4
BF = jnp.bfloat16
F32 = jnp.float32
AXES = ("zh", "zl", "xh", "y", "xl", "core")
FEAT = ("xl", "core")
BLK = ("zh", "zl", "xh", "y")


def exchange(pieces, axes):
    return lax.all_to_all(pieces, axes, 0, 0, tiled=True)


def share(piece, axes):
    count = lax.axis_size(axes)
    return exchange(jnp.broadcast_to(piece[None], (count,) + piece.shape), axes)


def mirror(piece):
    return lax.ppermute(piece, "zh", [(s, LAYERS - 1 - s) for s in range(LAYERS)])


def body(layer_inputs, mlp_targets, enc_weight, enc_bias, act_mask, dec_weight, owner_half):
    source = lax.axis_index("zh")
    side = owner_half[0]
    width = layer_inputs.shape[1]
    feats = enc_weight.shape[0]
    tokens = act_mask.shape[1]
    span = feats // 2
    parts = lax.axis_size(FEAT)
    quarter = span // parts
    part = lax.axis_index(FEAT)
    rows = layer_inputs.shape[0]
    zl, xy, zs = lax.axis_size("zl"), lax.axis_size(("xh", "y")), lax.axis_size(("zh", "zl"))

    own_inputs = share(layer_inputs, ("zl", "xh", "y")).reshape(tokens, width)
    pre_part = jnp.einsum("fd,md->fm", enc_weight, own_inputs, preferred_element_type=F32)
    pre_part = pre_part.astype(BF).reshape(2, parts, quarter, tokens).transpose(1, 0, 2, 3)
    pre = jnp.sum(exchange(pre_part, FEAT).astype(F32), axis=0)
    bias_q = lax.dynamic_index_in_dim(enc_bias.reshape(2, parts, quarter), part, 1, False)
    mask_q = lax.dynamic_index_in_dim(
        act_mask.reshape(2, parts, quarter, tokens), part, 1, False
    ).astype(F32)
    code_q = (mask_q * (pre + bias_q[:, :, None])).astype(BF)
    own_q = lax.dynamic_index_in_dim(code_q, side, 0, False)
    sent_q = lax.dynamic_index_in_dim(code_q, 1 - side, 0, False)
    both_q = jnp.stack([own_q, mirror(sent_q)])
    both = lax.all_gather(both_q, FEAT, axis=0)
    codes = both.transpose(1, 0, 2, 3).reshape(2, span, tokens)

    dec = dec_weight.reshape(LAYERS + 1, span, width)
    targets = jnp.arange(LAYERS)
    own_ok = targets >= source
    other_ok = targets >= LAYERS - 1 - source
    own_slot = jnp.where(own_ok, targets - source, 0)
    own_dec = jnp.take(dec, own_slot, axis=0)
    other_dec = dec[1:]
    own_codes = jnp.where(own_ok[:, None, None], codes[0][None], 0)
    other_codes = jnp.where(other_ok[:, None, None], codes[1][None], 0)
    pair_codes = jnp.concatenate([own_codes, other_codes], axis=1)
    pair_dec = jnp.concatenate([own_dec, other_dec], axis=1)
    recon_part = jnp.einsum("trm,trd->tmd", pair_codes, pair_dec, preferred_element_type=F32)
    pieces = recon_part.astype(BF).reshape(zs, xy, rows, width).transpose(1, 0, 2, 3)
    sums = jnp.sum(exchange(pieces, ("xh", "y")).astype(F32), axis=0).astype(BF)
    recon_rows = jnp.sum(exchange(sums, ("zh", "zl")).astype(F32), axis=0)
    error_rows = (recon_rows - mlp_targets.astype(F32)).astype(BF)
    error_z = share(error_rows, ("zh", "zl"))
    error = share(error_z, ("xh", "y"))
    error = error.transpose(1, 0, 2, 3).reshape(LAYERS, tokens, width)

    err_own = jnp.where(own_ok[:, None, None], error, 0)
    err_other = jnp.where(other_ok[:, None, None], error, 0)
    own_terms = jnp.einsum("trd,tmd->rm", own_dec, err_own, preferred_element_type=F32)
    other_terms = jnp.einsum("trd,tmd->rm", other_dec, err_other, preferred_element_type=F32)
    terms = jnp.stack([own_terms, other_terms]).astype(BF)
    terms = terms.reshape(2, parts, quarter, tokens).transpose(1, 0, 2, 3)
    terms_q = jnp.sum(exchange(terms, FEAT).astype(F32), axis=0)
    returned = mirror(terms_q[1].astype(BF)).astype(F32)
    grad_q = jnp.where(side == 0, jnp.stack([terms_q[0], returned]), jnp.stack([returned, terms_q[0]]))
    pre_grad_q = (mask_q * grad_q).astype(BF)
    pre_grad = lax.all_gather(pre_grad_q, FEAT, axis=0)
    pre_grad = pre_grad.transpose(1, 0, 2, 3).reshape(feats, tokens)
    bias_grad = jnp.sum(pre_grad.astype(F32), axis=1)
    enc_grad = jnp.einsum("fm,md->fd", pre_grad, own_inputs, preferred_element_type=F32)

    slots = jnp.arange(LAYERS + 1)
    slot_own = slots < LAYERS - source
    slot_target = jnp.where(slot_own, source + slots, slots - 1)
    slot_codes = jnp.where(slot_own[:, None, None], codes[0][None], codes[1][None])
    slot_err = jnp.take(error, slot_target, axis=0)
    dec_grad = jnp.einsum("jrm,jmd->jrd", slot_codes, slot_err, preferred_element_type=F32)
    dec_out = dec_grad.astype(BF).reshape(dec_weight.shape)
    return (recon_rows.astype(BF), enc_grad.astype(BF), bias_grad, dec_out)


def solution(mesh):
    fine = Mesh(mesh.devices.reshape(LAYERS, 4, 2, 4, 2, 2), AXES)
    wide = P(BLK, FEAT)
    in_specs = (wide, wide, wide, P(BLK), P(BLK, None), wide, P(BLK))
    out_specs = (wide, wide, P(BLK), wide)
    return jax.shard_map(body, mesh=fine, in_specs=in_specs, out_specs=out_specs, check_vma=False)
```

```python
import jax
import jax.numpy as jnp
from jax import lax
from jax.experimental import pallas as pl
from jax.experimental.pallas import tpu as pltpu
from jax.sharding import Mesh, PartitionSpec as P

LAYERS = 4
BF = jnp.bfloat16
F32 = jnp.float32
AXES = ("zh", "zm", "zb", "xh", "y", "xl", "core")
NEAR = ("zb", "xh", "y")
FAR = ("zh", "zm")
FEAT = ("xl", "core")
BLK = ("zh", "zm", "zb", "xh", "y")
VMEM_BYTES = 40 * 1024 * 1024


def exchange(pieces, axes):
    return lax.all_to_all(pieces, axes, 0, 0, tiled=True)


def share(piece, axes):
    count = lax.axis_size(axes)
    return exchange(jnp.broadcast_to(piece[None], (count,) + piece.shape), axes)


def mirror(piece):
    return lax.ppermute(piece, "zh", [(s, LAYERS - 1 - s) for s in range(LAYERS)])


def own_slot(source, target):
    return pl.multiple_of(jnp.maximum(target - source, 0) * 256, 256)


def recon_kernel(source_ref, codes_ref, dec_ref, out_ref):
    source = source_ref[0]
    groups, _, rows, width = out_ref.shape
    span = codes_ref.shape[1] // 2
    for target in range(LAYERS):
        own = jnp.where(target >= source, codes_ref[:, :span], 0)
        other = jnp.where(target >= LAYERS - 1 - source, codes_ref[:, span:], 0)
        own_dec = dec_ref[:, pl.ds(own_slot(source, target), span)]
        other_dec = dec_ref[:, (target + 1) * span : (target + 2) * span]
        dims = (((1,), (1,)), ((), ()))
        total = lax.dot_general(own.astype(BF), own_dec, dims, preferred_element_type=F32)
        total += lax.dot_general(other.astype(BF), other_dec, dims, preferred_element_type=F32)
        out_ref[:, target] = total.astype(BF).reshape(groups, rows, width)


def terms_kernel(source_ref, error_ref, dec_ref, out_ref):
    source = source_ref[0]
    width = error_ref.shape[3]
    tokens, both = out_ref.shape
    span = both // 2
    own_sum = jnp.zeros((tokens, span), F32)
    other_sum = jnp.zeros((tokens, span), F32)
    for target in range(LAYERS):
        error = error_ref[:, target].reshape(tokens, width)
        own_dec = dec_ref[:, pl.ds(own_slot(source, target), span)]
        other_dec = dec_ref[:, (target + 1) * span : (target + 2) * span]
        own = jnp.dot(error, own_dec, preferred_element_type=F32)
        other = jnp.dot(error, other_dec, preferred_element_type=F32)
        own_sum += jnp.where(target >= source, own, 0.0)
        other_sum += jnp.where(target >= LAYERS - 1 - source, other, 0.0)
    out_ref[:, :span] = own_sum.astype(BF)
    out_ref[:, span:] = other_sum.astype(BF)


def dec_grad_kernel(source_ref, error_ref, codes_ref, out_ref):
    source = source_ref[0]
    width = error_ref.shape[3]
    tokens, both = codes_ref.shape
    span = both // 2
    for slot in range(LAYERS + 1):
        is_own = slot < LAYERS - source
        target = jnp.where(is_own, source + slot, slot - 1)
        error = error_ref[:, pl.ds(target, 1)].reshape(tokens, width)
        codes = jnp.where(is_own, codes_ref[:, :span], codes_ref[:, span:])
        grad = lax.dot_general(
            error, codes, (((0,), (0,)), ((), ())), preferred_element_type=F32
        )
        out_ref[:, slot * span : (slot + 1) * span] = grad.astype(BF)


def call(kernel, shape, flops, moved, *operands):
    specs = [pl.BlockSpec(memory_space=pltpu.SMEM)]
    specs += [pl.BlockSpec(memory_space=pltpu.VMEM)] * (len(operands) - 1)
    return pl.pallas_call(
        kernel,
        out_shape=jax.ShapeDtypeStruct(shape, BF),
        in_specs=specs,
        out_specs=pl.BlockSpec(memory_space=pltpu.VMEM),
        compiler_params=pltpu.CompilerParams(vmem_limit_bytes=VMEM_BYTES),
        cost_estimate=pl.CostEstimate(flops=flops, bytes_accessed=moved, transcendentals=0),
    )(*operands)


def body(layer_inputs, mlp_targets, enc_weight, enc_bias, act_mask, dec_weight, owner_half):
    source = lax.axis_index("zh").astype(jnp.int32).reshape(1)
    first = owner_half[0] == 0
    rows, width = layer_inputs.shape
    feats, tokens = act_mask.shape
    span = feats // 2
    parts = lax.axis_size(FEAT)
    near, far = lax.axis_size(NEAR), lax.axis_size(FAR)
    zm = lax.axis_size("zm")
    quarter = tokens // parts

    place = lax.axis_index(FEAT) * quarter + jnp.arange(quarter)
    token = place // rows % zm * (near * rows) + place // (rows * zm) * rows + place % rows
    picked = (token[:, None] == jnp.arange(tokens)[None, :]).astype(BF)
    mask_q = jnp.einsum("qm,fm->qf", picked, act_mask.astype(BF), preferred_element_type=F32)
    dec = dec_weight.T

    own_inputs = share(layer_inputs, NEAR + ("zm",)).reshape(tokens, width)
    pre_part = jnp.einsum("md,fd->mf", own_inputs, enc_weight, preferred_element_type=F32)
    pre_part = pre_part.astype(BF).reshape(parts, quarter, feats)
    pre = jnp.sum(exchange(pre_part, FEAT).astype(F32), axis=0) + enc_bias[None, :]
    code_q = (mask_q * pre).astype(BF)
    low, high = code_q[:, :span], code_q[:, span:]
    received = mirror(jnp.where(first, high, low))
    both_q = jnp.concatenate([jnp.where(first, low, high), received], axis=1)
    codes = lax.all_gather(both_q, FEAT, axis=0, tiled=True)

    pieces = call(
        recon_kernel, (near, LAYERS, zm * rows, width), 8 * 2 * tokens * span * width, 3000000,
        source, codes, dec,
    )
    sums = jnp.sum(exchange(pieces, NEAR).astype(F32), axis=0).astype(BF)
    sums = sums.reshape(far, rows, width)
    recon_rows = jnp.sum(exchange(sums, FAR).astype(F32), axis=0)
    error_rows = (recon_rows - mlp_targets.astype(F32)).astype(BF)
    error = share(error_rows, FAR).reshape(LAYERS, zm * rows, width)
    error = share(error, NEAR).reshape(near, LAYERS, zm * rows, width)

    terms = call(
        terms_kernel, (tokens, feats), 8 * 2 * tokens * span * width, 3000000,
        source, error, dec,
    )
    terms = exchange(terms.reshape(parts, quarter, feats), FEAT)
    terms_q = jnp.sum(terms.astype(F32), axis=0)
    returned = mirror(terms_q[:, span:].astype(BF)).astype(F32)
    own = terms_q[:, :span]
    grad_q = jnp.concatenate(
        [jnp.where(first, own, returned), jnp.where(first, returned, own)], axis=1
    )
    pre_grad = lax.all_gather((mask_q * grad_q).astype(BF), FEAT, axis=0, tiled=True)
    bias_grad = jnp.sum(pre_grad.astype(F32), axis=0)
    enc_grad = jnp.einsum("mf,md->fd", pre_grad, own_inputs, preferred_element_type=F32)
    dec_grad = call(
        dec_grad_kernel, dec.shape, 5 * 2 * tokens * span * width, 3000000,
        source, error, codes,
    )
    return (recon_rows.astype(BF), enc_grad.astype(BF), bias_grad, dec_grad.T)


def solution(mesh):
    fine = Mesh(mesh.devices.reshape(LAYERS, 2, 2, 2, 4, 2, 2), AXES)
    wide = P(BLK, FEAT)
    in_specs = (wide, wide, wide, P(BLK), P(BLK, None), wide, P(BLK))
    out_specs = (wide, wide, P(BLK), wide)
    return jax.shard_map(body, mesh=fine, in_specs=in_specs, out_specs=out_specs, check_vma=False)
```

```python
import jax
import jax.numpy as jnp
from jax import lax
from jax.experimental import pallas as pl
from jax.experimental.pallas import tpu as pltpu
from jax.sharding import Mesh, PartitionSpec as P

LAYERS = 4
BF = jnp.bfloat16
F32 = jnp.float32
AXES = ("zh", "zm", "zb", "xh", "y", "xl", "core")
NEAR = ("zb", "xh", "y")
FAR = ("zh", "zm")
FEAT = ("xl", "core")
BLK = ("zh", "zm", "zb", "xh", "y")
VMEM_BYTES = 16 * 1024 * 1024


def exchange(pieces, axes):
    return lax.all_to_all(pieces, axes, 0, 0, tiled=True)


def share(piece, axes):
    count = lax.axis_size(axes)
    return exchange(jnp.broadcast_to(piece[None], (count,) + piece.shape), axes)


def mirror(piece):
    return lax.ppermute(piece, "zh", [(s, LAYERS - 1 - s) for s in range(LAYERS)])


def array(shape, dtype=BF):
    return jax.ShapeDtypeStruct(shape, dtype)


def own_slot(source, target):
    return pl.multiple_of(jnp.maximum(target - source, 0) * 256, 256)


def recon_kernel(source_ref, codes_ref, dec_ref, out_ref):
    source = source_ref[0]
    groups, _, rows, width = out_ref.shape
    span = codes_ref.shape[1] // 2
    for target in range(LAYERS):
        own = jnp.where(target >= source, codes_ref[:, :span], 0)
        other = jnp.where(target >= LAYERS - 1 - source, codes_ref[:, span:], 0)
        own_dec = dec_ref[:, pl.ds(own_slot(source, target), span)]
        other_dec = dec_ref[:, (target + 1) * span : (target + 2) * span]
        dims = (((1,), (1,)), ((), ()))
        total = lax.dot_general(own.astype(BF), own_dec, dims, preferred_element_type=F32)
        total += lax.dot_general(other.astype(BF), other_dec, dims, preferred_element_type=F32)
        out_ref[:, target] = total.astype(BF).reshape(groups, rows, width)


def terms_kernel(source_ref, error_ref, dec_ref, out_ref):
    source = source_ref[0]
    width = error_ref.shape[3]
    tokens, both = out_ref.shape
    span = both // 2
    own_sum = jnp.zeros((tokens, span), F32)
    other_sum = jnp.zeros((tokens, span), F32)
    for target in range(LAYERS):
        error = error_ref[:, target].reshape(tokens, width)
        own_dec = dec_ref[:, pl.ds(own_slot(source, target), span)]
        other_dec = dec_ref[:, (target + 1) * span : (target + 2) * span]
        own = jnp.dot(error, own_dec, preferred_element_type=F32)
        other = jnp.dot(error, other_dec, preferred_element_type=F32)
        own_sum += jnp.where(target >= source, own, 0.0)
        other_sum += jnp.where(target >= LAYERS - 1 - source, other, 0.0)
    out_ref[:, :span] = own_sum.astype(BF)
    out_ref[:, span:] = other_sum.astype(BF)


def dec_grad_kernel(source_ref, error_ref, codes_ref, out_ref):
    source = source_ref[0]
    width = error_ref.shape[3]
    tokens, both = codes_ref.shape
    span = both // 2
    for slot in range(LAYERS + 1):
        is_own = slot < LAYERS - source
        target = jnp.where(is_own, source + slot, slot - 1)
        error = error_ref[:, pl.ds(target, 1)].reshape(tokens, width)
        codes = jnp.where(is_own, codes_ref[:, :span], codes_ref[:, span:])
        grad = lax.dot_general(
            error, codes, (((0,), (0,)), ((), ())), preferred_element_type=F32
        )
        out_ref[:, slot * span : (slot + 1) * span] = grad.astype(BF)


def pre_kernel(inputs_ref, weight_ref, out_ref):
    pre = jnp.dot(inputs_ref[...], weight_ref[...], preferred_element_type=F32)
    out_ref[...] = pre.astype(BF)


def sum_kernel(pieces_ref, out_ref):
    for target in range(LAYERS):
        out_ref[target] = jnp.sum(pieces_ref[:, target].astype(F32), axis=0).astype(BF)


def enc_grad_kernel(inputs_ref, grad_ref, out_ref, bias_ref):
    grad = grad_ref[...]
    total = lax.dot_general(
        inputs_ref[...], grad, (((0,), (0,)), ((), ())), preferred_element_type=F32
    )
    out_ref[...] = total.astype(BF)
    bias_ref[...] = jnp.sum(grad.astype(F32), axis=0, keepdims=True)


def call(kernel, shapes, flops, moved, *operands):
    where = [pltpu.SMEM if operand.dtype == jnp.int32 else pltpu.VMEM for operand in operands]
    outs = jax.tree.map(lambda _: pl.BlockSpec(memory_space=pltpu.VMEM), shapes)
    return pl.pallas_call(
        kernel,
        out_shape=shapes,
        in_specs=[pl.BlockSpec(memory_space=space) for space in where],
        out_specs=outs,
        compiler_params=pltpu.CompilerParams(vmem_limit_bytes=VMEM_BYTES),
        cost_estimate=pl.CostEstimate(flops=flops, bytes_accessed=moved, transcendentals=0),
    )(*operands)


def body(layer_inputs, mlp_targets, enc_weight, enc_bias, act_mask, dec_weight, owner_half):
    source = lax.axis_index("zh").astype(jnp.int32).reshape(1)
    first = owner_half[0] == 0
    rows, width = layer_inputs.shape
    feats, tokens = act_mask.shape
    span = feats // 2
    parts = lax.axis_size(FEAT)
    near, far = lax.axis_size(NEAR), lax.axis_size(FAR)
    zm = lax.axis_size("zm")
    quarter = tokens // parts

    place = lax.axis_index(FEAT) * quarter + jnp.arange(quarter)
    token = place // rows % zm * (near * rows) + place // (rows * zm) * rows + place % rows
    picked = (token[:, None] == jnp.arange(tokens)[None, :]).astype(BF)
    mask_q = jnp.einsum("qm,fm->qf", picked, act_mask.astype(BF), preferred_element_type=F32)
    dec = dec_weight.T

    own_inputs = share(layer_inputs, NEAR + ("zm",)).reshape(tokens, width)
    pre_part = call(
        pre_kernel, array((tokens, feats)), 2 * tokens * feats * width, 1200000,
        own_inputs, enc_weight.T,
    ).reshape(parts, quarter, feats)
    pre = jnp.sum(exchange(pre_part, FEAT).astype(F32), axis=0) + enc_bias[None, :]
    code_q = (mask_q * pre).astype(BF)
    low, high = code_q[:, :span], code_q[:, span:]
    received = mirror(jnp.where(first, high, low))
    both_q = jnp.concatenate([jnp.where(first, low, high), received], axis=1)
    codes = lax.all_gather(both_q, FEAT, axis=0, tiled=True)

    pieces = call(
        recon_kernel, array((near, LAYERS, zm * rows, width)), 8 * 2 * tokens * span * width, 3000000,
        source, codes, dec,
    )
    sums = call(
        sum_kernel, array((LAYERS, zm * rows, width)), tokens * LAYERS * width, 1300000,
        exchange(pieces, NEAR),
    ).reshape(far, rows, width)
    recon_rows = jnp.sum(exchange(sums, FAR).astype(F32), axis=0)
    error_rows = (recon_rows - mlp_targets.astype(F32)).astype(BF)
    error = share(error_rows, FAR).reshape(LAYERS, zm * rows, width)
    error = share(error, NEAR).reshape(near, LAYERS, zm * rows, width)

    terms = call(
        terms_kernel, array((tokens, feats)), 8 * 2 * tokens * span * width, 3000000,
        source, error, dec,
    )
    terms = exchange(terms.reshape(parts, quarter, feats), FEAT)
    terms_q = jnp.sum(terms.astype(F32), axis=0)
    terms_q, recon_rows = lax.optimization_barrier((terms_q, recon_rows))
    returned = mirror(terms_q[:, span:].astype(BF)).astype(F32)
    own = terms_q[:, :span]
    grad_q = jnp.concatenate(
        [jnp.where(first, own, returned), jnp.where(first, returned, own)], axis=1
    )
    pre_grad = lax.all_gather((mask_q * grad_q).astype(BF), FEAT, axis=0, tiled=True)
    enc_grad, bias_grad = call(
        enc_grad_kernel, (array((width, feats)), array((1, feats), F32)),
        2 * tokens * feats * width, 1200000, own_inputs, pre_grad,
    )
    dec_grad = call(
        dec_grad_kernel, array(dec.shape), 5 * 2 * tokens * span * width, 3000000,
        source, error, codes,
    )
    return (recon_rows.astype(BF), enc_grad.T, bias_grad[0], dec_grad.T)


def solution(mesh):
    fine = Mesh(mesh.devices.reshape(LAYERS, 2, 2, 2, 4, 2, 2), AXES)
    wide = P(BLK, FEAT)
    in_specs = (wide, wide, wide, P(BLK), P(BLK, None), wide, P(BLK))
    out_specs = (wide, wide, P(BLK), wide)
    return jax.shard_map(body, mesh=fine, in_specs=in_specs, out_specs=out_specs, check_vma=False)
```

```python
import jax
import jax.numpy as jnp
from jax import lax
from jax.experimental import pallas as pl
from jax.experimental.pallas import tpu as pltpu
from jax.sharding import Mesh, PartitionSpec as P

LAYERS = 4
BF = jnp.bfloat16
F32 = jnp.float32
AXES = ("zh", "zm", "zb", "xh", "y", "xl", "core")
NEAR = ("zb", "xh", "y")
FEAT = ("xl", "core")
BLK = ("zh", "zm", "zb", "xh", "y")
VMEM_BYTES = 16 * 1024 * 1024


def exchange(pieces, axes):
    return lax.all_to_all(pieces, axes, 0, 0, tiled=True)


def share(piece, axes):
    count = lax.axis_size(axes)
    return exchange(jnp.broadcast_to(piece[None], (count,) + piece.shape), axes)


MIRRORED = [[0, 3], [1, 2]]
ADJACENT = [[0, 1], [2, 3]]


def mirror(piece):
    return lax.ppermute(piece, "zh", [(s, LAYERS - 1 - s) for s in range(LAYERS)])


def both_of(piece, pairs):
    layer = lax.axis_index("zh")
    second = sum((layer == pair[1]).astype(jnp.int32) for pair in pairs)
    return lax.all_gather(piece, "zh", axis=0, axis_index_groups=pairs), 1 - second


def pick(pair, place):
    return jnp.where(place == 0, pair[0], pair[1])


def array(shape, dtype=BF):
    return jax.ShapeDtypeStruct(shape, dtype)


def own_slot(source, target):
    return pl.multiple_of(jnp.maximum(target - source, 0) * 256, 256)


def recon_kernel(source_ref, codes_ref, dec_ref, out_ref):
    source = source_ref[0]
    groups, _, rows, width = out_ref.shape
    span = codes_ref.shape[1] // 2
    for target in range(LAYERS):
        own = jnp.where(target >= source, codes_ref[:, :span], 0)
        other = jnp.where(target >= LAYERS - 1 - source, codes_ref[:, span:], 0)
        own_dec = dec_ref[:, pl.ds(own_slot(source, target), span)]
        other_dec = dec_ref[:, (target + 1) * span : (target + 2) * span]
        dims = (((1,), (1,)), ((), ()))
        total = lax.dot_general(own.astype(BF), own_dec, dims, preferred_element_type=F32)
        total += lax.dot_general(other.astype(BF), other_dec, dims, preferred_element_type=F32)
        out_ref[:, target] = total.astype(BF).reshape(groups, rows, width)


def terms_kernel(source_ref, error_ref, dec_ref, out_ref):
    source = source_ref[0]
    width = error_ref.shape[3]
    tokens, both = out_ref.shape
    span = both // 2
    own_sum = jnp.zeros((tokens, span), F32)
    other_sum = jnp.zeros((tokens, span), F32)
    for target in range(LAYERS):
        error = error_ref[:, target].reshape(tokens, width)
        own_dec = dec_ref[:, pl.ds(own_slot(source, target), span)]
        other_dec = dec_ref[:, (target + 1) * span : (target + 2) * span]
        own = jnp.dot(error, own_dec, preferred_element_type=F32)
        other = jnp.dot(error, other_dec, preferred_element_type=F32)
        own_sum += jnp.where(target >= source, own, 0.0)
        other_sum += jnp.where(target >= LAYERS - 1 - source, other, 0.0)
    out_ref[:, :span] = own_sum.astype(BF)
    out_ref[:, span:] = other_sum.astype(BF)


def dec_grad_kernel(source_ref, error_ref, codes_ref, out_ref):
    source = source_ref[0]
    width = error_ref.shape[3]
    tokens, both = codes_ref.shape
    span = both // 2
    for slot in range(LAYERS + 1):
        is_own = slot < LAYERS - source
        target = jnp.where(is_own, source + slot, slot - 1)
        error = error_ref[:, pl.ds(target, 1)].reshape(tokens, width)
        codes = jnp.where(is_own, codes_ref[:, :span], codes_ref[:, span:])
        grad = lax.dot_general(
            error, codes, (((0,), (0,)), ((), ())), preferred_element_type=F32
        )
        out_ref[:, slot * span : (slot + 1) * span] = grad.astype(BF)


def pre_kernel(inputs_ref, weight_ref, out_ref):
    pre = jnp.dot(inputs_ref[...], weight_ref[...], preferred_element_type=F32)
    out_ref[...] = pre.astype(BF)


def sum_kernel(pieces_ref, out_ref):
    for target in range(LAYERS):
        out_ref[target] = jnp.sum(pieces_ref[:, target].astype(F32), axis=0)


def enc_grad_kernel(inputs_ref, grad_ref, out_ref, bias_ref):
    grad = grad_ref[...]
    total = lax.dot_general(
        inputs_ref[...], grad, (((0,), (0,)), ((), ())), preferred_element_type=F32
    )
    out_ref[...] = total.astype(BF)
    bias_ref[...] = jnp.sum(grad.astype(F32), axis=0, keepdims=True)


def call(kernel, shapes, flops, moved, *operands):
    where = [pltpu.SMEM if operand.dtype == jnp.int32 else pltpu.VMEM for operand in operands]
    outs = jax.tree.map(lambda _: pl.BlockSpec(memory_space=pltpu.VMEM), shapes)
    return pl.pallas_call(
        kernel,
        out_shape=shapes,
        in_specs=[pl.BlockSpec(memory_space=space) for space in where],
        out_specs=outs,
        compiler_params=pltpu.CompilerParams(vmem_limit_bytes=VMEM_BYTES),
        cost_estimate=pl.CostEstimate(flops=flops, bytes_accessed=moved, transcendentals=0),
    )(*operands)


def body(layer_inputs, mlp_targets, enc_weight, enc_bias, act_mask, dec_weight, owner_half):
    source = lax.axis_index("zh").astype(jnp.int32).reshape(1)
    first = owner_half[0] == 0
    rows, width = layer_inputs.shape
    feats, tokens = act_mask.shape
    span = feats // 2
    parts = lax.axis_size(FEAT)
    near = lax.axis_size(NEAR)
    zm = lax.axis_size("zm")
    quarter = tokens // parts

    place = lax.axis_index(FEAT) * quarter + jnp.arange(quarter)
    token = place // rows % zm * (near * rows) + place // (rows * zm) * rows + place % rows
    picked = (token[:, None] == jnp.arange(tokens)[None, :]).astype(BF)
    mask_q = jnp.einsum("qm,fm->qf", picked, act_mask.astype(BF), preferred_element_type=F32)
    dec = dec_weight.T

    own_inputs = share(layer_inputs, NEAR + ("zm",)).reshape(tokens, width)
    pre_part = call(
        pre_kernel, array((tokens, feats)), 2 * tokens * feats * width, 1200000,
        own_inputs, enc_weight.T,
    ).reshape(parts, quarter, feats)
    pre = jnp.sum(exchange(pre_part, FEAT).astype(F32), axis=0) + enc_bias[None, :]
    code_q = (mask_q * pre).astype(BF)
    low, high = code_q[:, :span], code_q[:, span:]
    received = pick(*both_of(jnp.where(first, high, low), MIRRORED))
    both_q = jnp.concatenate([jnp.where(first, low, high), received], axis=1)
    codes = lax.all_gather(both_q, FEAT, axis=0, tiled=True)

    pieces = call(
        recon_kernel, array((near, LAYERS, zm * rows, width)), 8 * 2 * tokens * span * width, 3000000,
        source, codes, dec,
    )
    block = (LAYERS, zm, rows, width)
    sums = call(
        sum_kernel, array((LAYERS, zm * rows, width), F32), tokens * LAYERS * width, 1400000,
        exchange(pieces, NEAR),
    ).reshape(block)
    sums, targets = lax.optimization_barrier((sums, mlp_targets))
    layer, place = lax.axis_index("zh"), lax.axis_index("zm")
    mine = jnp.arange(LAYERS)[:, None] == layer
    mine = (mine & (jnp.arange(zm)[None, :] == place))[:, :, None, None]
    part = (sums - jnp.where(mine, targets.astype(F32)[None, None], 0.0)).astype(BF)

    def own_rows(array):
        return lax.dynamic_slice(array, (layer, place, 0, 0), (1, 1, rows, width))[0, 0]

    near_pair = lax.all_gather(part.reshape(LAYERS, zm * rows, width), "zm", axis=0)
    arrived = [(near_pair, 1 - place)]
    part = jnp.sum(near_pair.astype(F32), axis=0).astype(BF)
    for pairs in (MIRRORED, ADJACENT):
        pair, other = both_of(part, pairs)
        arrived.append((pair, other))
        part = jnp.sum(pair.astype(F32), axis=0).astype(BF)
    error = part
    error = share(error, NEAR).reshape(near, LAYERS, zm * rows, width)

    terms = call(
        terms_kernel, array((tokens, feats)), 8 * 2 * tokens * span * width, 3000000,
        source, error, dec,
    )
    terms = exchange(terms.reshape(parts, quarter, feats), FEAT)
    terms_q = jnp.sum(terms.astype(F32), axis=0)
    terms_q, sums, arrived = lax.optimization_barrier((terms_q, sums, arrived))
    recon_rows = own_rows(sums)
    for pair, other in arrived:
        recon_rows += own_rows(pick(pair, other).reshape(block)).astype(F32)
    returned = mirror(terms_q[:, span:].astype(BF)).astype(F32)
    own = terms_q[:, :span]
    grad_q = jnp.concatenate(
        [jnp.where(first, own, returned), jnp.where(first, returned, own)], axis=1
    )
    pre_grad = lax.all_gather((mask_q * grad_q).astype(BF), FEAT, axis=0, tiled=True)
    enc_grad, bias_grad = call(
        enc_grad_kernel, (array((width, feats)), array((1, feats), F32)),
        2 * tokens * feats * width, 1200000, own_inputs, pre_grad,
    )
    dec_grad = call(
        dec_grad_kernel, array(dec.shape), 5 * 2 * tokens * span * width, 3000000,
        source, error, codes,
    )
    return (recon_rows.astype(BF), enc_grad.T, bias_grad[0], dec_grad.T)


def solution(mesh):
    fine = Mesh(mesh.devices.reshape(LAYERS, 2, 2, 2, 4, 2, 2), AXES)
    wide = P(BLK, FEAT)
    in_specs = (wide, wide, wide, P(BLK), P(BLK, None), wide, P(BLK))
    out_specs = (wide, wide, P(BLK), wide)
    return jax.shard_map(body, mesh=fine, in_specs=in_specs, out_specs=out_specs, check_vma=False)
```

```python
import jax
import jax.numpy as jnp
from jax import lax
from jax.experimental import pallas as pl
from jax.experimental.pallas import tpu as pltpu
from jax.sharding import Mesh, PartitionSpec as P

LAYERS = 4
BF = jnp.bfloat16
F32 = jnp.float32
AXES = ("zh", "zm", "zb", "xh", "y", "xl", "core")
NEAR = ("zb", "xh", "y")
FEAT = ("xl", "core")
BLK = ("zh", "zm", "zb", "xh", "y")
VMEM_BYTES = 16 * 1024 * 1024


def exchange(pieces, axes):
    return lax.all_to_all(pieces, axes, 0, 0, tiled=True)


def share(piece, axes):
    count = lax.axis_size(axes)
    return exchange(jnp.broadcast_to(piece[None], (count,) + piece.shape), axes)


MIRRORED = [[0, 3], [1, 2]]
ADJACENT = [[0, 1], [2, 3]]


def mirror(piece):
    return lax.ppermute(piece, "zh", [(s, LAYERS - 1 - s) for s in range(LAYERS)])


def both_of(piece, pairs, layer):
    second = sum((layer == pair[1]).astype(jnp.int32) for pair in pairs)
    return lax.all_gather(piece, "zh", axis=0, axis_index_groups=pairs), 1 - second


def pick(pair, place):
    return jnp.where(place == 0, pair[0], pair[1])


def array(shape, dtype=BF):
    return jax.ShapeDtypeStruct(shape, dtype)


def own_slot(source, target):
    return pl.multiple_of(jnp.maximum(target - source, 0) * 256, 256)


def recon_kernel(source_ref, codes_ref, dec_ref, out_ref):
    source = source_ref[0]
    groups, _, rows, width = out_ref.shape
    span = codes_ref.shape[1] // 2
    for target in range(LAYERS):
        own = jnp.where(target >= source, codes_ref[:, :span], 0)
        other = jnp.where(target >= LAYERS - 1 - source, codes_ref[:, span:], 0)
        own_dec = dec_ref[:, pl.ds(own_slot(source, target), span)]
        other_dec = dec_ref[:, (target + 1) * span : (target + 2) * span]
        dims = (((1,), (1,)), ((), ()))
        total = lax.dot_general(own.astype(BF), own_dec, dims, preferred_element_type=F32)
        total += lax.dot_general(other.astype(BF), other_dec, dims, preferred_element_type=F32)
        out_ref[:, target] = total.astype(BF).reshape(groups, rows, width)


def terms_kernel(source_ref, error_ref, dec_ref, out_ref):
    source = source_ref[0]
    width = error_ref.shape[3]
    tokens, both = out_ref.shape
    span = both // 2
    own_sum = jnp.zeros((tokens, span), F32)
    other_sum = jnp.zeros((tokens, span), F32)
    for target in range(LAYERS):
        error = error_ref[:, target].reshape(tokens, width)
        own_dec = dec_ref[:, pl.ds(own_slot(source, target), span)]
        other_dec = dec_ref[:, (target + 1) * span : (target + 2) * span]
        own = jnp.dot(error, own_dec, preferred_element_type=F32)
        other = jnp.dot(error, other_dec, preferred_element_type=F32)
        own_sum += jnp.where(target >= source, own, 0.0)
        other_sum += jnp.where(target >= LAYERS - 1 - source, other, 0.0)
    out_ref[:, :span] = own_sum.astype(BF)
    out_ref[:, span:] = other_sum.astype(BF)


def dec_grad_kernel(source_ref, error_ref, codes_ref, out_ref):
    source = source_ref[0]
    width = error_ref.shape[3]
    tokens, both = codes_ref.shape
    span = both // 2
    for slot in range(LAYERS + 1):
        is_own = slot < LAYERS - source
        target = jnp.where(is_own, source + slot, slot - 1)
        error = error_ref[:, pl.ds(target, 1)].reshape(tokens, width)
        codes = jnp.where(is_own, codes_ref[:, :span], codes_ref[:, span:])
        grad = lax.dot_general(
            error, codes, (((0,), (0,)), ((), ())), preferred_element_type=F32
        )
        out_ref[:, slot * span : (slot + 1) * span] = grad.astype(BF)


def pre_kernel(inputs_ref, weight_ref, out_ref):
    pre = jnp.dot(inputs_ref[...], weight_ref[...], preferred_element_type=F32)
    out_ref[...] = pre.astype(BF)


def sum_kernel(pieces_ref, out_ref):
    for target in range(LAYERS):
        out_ref[target] = jnp.sum(pieces_ref[:, target].astype(F32), axis=0)


def enc_grad_kernel(inputs_ref, grad_ref, out_ref, bias_ref):
    grad = grad_ref[...]
    total = lax.dot_general(
        inputs_ref[...], grad, (((0,), (0,)), ((), ())), preferred_element_type=F32
    )
    out_ref[...] = total.astype(BF)
    bias_ref[...] = jnp.sum(grad.astype(F32), axis=0, keepdims=True)


def call(kernel, shapes, flops, moved, *operands):
    where = [pltpu.SMEM if operand.dtype == jnp.int32 else pltpu.VMEM for operand in operands]
    outs = jax.tree.map(lambda _: pl.BlockSpec(memory_space=pltpu.VMEM), shapes)
    return pl.pallas_call(
        kernel,
        out_shape=shapes,
        in_specs=[pl.BlockSpec(memory_space=space) for space in where],
        out_specs=outs,
        compiler_params=pltpu.CompilerParams(vmem_limit_bytes=VMEM_BYTES),
        cost_estimate=pl.CostEstimate(flops=flops, bytes_accessed=moved, transcendentals=0),
    )(*operands)


def body(layer_inputs, mlp_targets, enc_weight, enc_bias, act_mask, dec_weight, owner_half):
    source = lax.axis_index("zh").astype(jnp.int32).reshape(1)
    first = owner_half[0] == 0
    rows, width = layer_inputs.shape
    feats, tokens = act_mask.shape
    span = feats // 2
    parts = lax.axis_size(FEAT)
    near = lax.axis_size(NEAR)
    zm = lax.axis_size("zm")
    quarter = tokens // parts

    place = lax.axis_index(FEAT) * quarter + jnp.arange(quarter)
    token = place // rows % zm * (near * rows) + place // (rows * zm) * rows + place % rows
    picked = (token[:, None] == jnp.arange(tokens)[None, :]).astype(BF)
    mask_q = jnp.einsum("qm,fm->qf", picked, act_mask.astype(BF), preferred_element_type=F32)
    dec = dec_weight.T

    own_inputs = share(layer_inputs, NEAR + ("zm",)).reshape(tokens, width)
    pre_part = call(
        pre_kernel, array((tokens, feats)), 2 * tokens * feats * width, 1200000,
        own_inputs, enc_weight.T,
    ).reshape(parts, quarter, feats)
    pre = jnp.sum(exchange(pre_part, FEAT).astype(F32), axis=0) + enc_bias[None, :]
    code_q = (mask_q * pre).astype(BF)
    low, high = code_q[:, :span], code_q[:, span:]
    received = pick(*both_of(jnp.where(first, high, low), MIRRORED, source[0]))
    both_q = jnp.concatenate([jnp.where(first, low, high), received], axis=1)
    codes = lax.all_gather(both_q, FEAT, axis=0, tiled=True)

    pieces = call(
        recon_kernel, array((near, LAYERS, zm * rows, width)), 8 * 2 * tokens * span * width, 3000000,
        source, codes, dec,
    )
    block = (LAYERS, zm, rows, width)
    sums = call(
        sum_kernel, array((LAYERS, zm * rows, width), F32), tokens * LAYERS * width, 1400000,
        exchange(pieces, NEAR),
    ).reshape(block)
    layer, place = lax.axis_index("zh"), lax.axis_index("zm")
    sums, targets, layer, place = lax.optimization_barrier((sums, mlp_targets, layer, place))
    mine = jnp.arange(LAYERS)[:, None] == layer
    mine = (mine & (jnp.arange(zm)[None, :] == place))[:, :, None, None]
    part = (sums - jnp.where(mine, targets.astype(F32)[None, None], 0.0)).astype(BF)

    def own_rows(array):
        return lax.dynamic_slice(array, (layer, place, 0, 0), (1, 1, rows, width))[0, 0]

    near_pair = lax.all_gather(part.reshape(LAYERS, zm * rows, width), "zm", axis=0)
    arrived = [(near_pair, 1 - place)]
    part = jnp.sum(near_pair.astype(F32), axis=0).astype(BF)
    for pairs in (MIRRORED, ADJACENT):
        pair, other = both_of(part, pairs, layer)
        arrived.append((pair, other))
        part = jnp.sum(pair.astype(F32), axis=0).astype(BF)
    error = part
    error = share(error, NEAR).reshape(near, LAYERS, zm * rows, width)

    terms = call(
        terms_kernel, array((tokens, feats)), 8 * 2 * tokens * span * width, 3000000,
        source, error, dec,
    )
    terms = exchange(terms.reshape(parts, quarter, feats), FEAT)
    terms_q = jnp.sum(terms.astype(F32), axis=0)
    late = (terms_q, sums, arrived, error, codes)
    terms_q, sums, arrived, error, codes = lax.optimization_barrier(late)
    recon_rows = own_rows(sums)
    for pair, other in arrived:
        recon_rows += own_rows(pick(pair, other).reshape(block)).astype(F32)
    returned = mirror(terms_q[:, span:].astype(BF)).astype(F32)
    own = terms_q[:, :span]
    grad_q = jnp.concatenate(
        [jnp.where(first, own, returned), jnp.where(first, returned, own)], axis=1
    )
    pre_grad = lax.all_gather((mask_q * grad_q).astype(BF), FEAT, axis=0, tiled=True)
    enc_grad, bias_grad = call(
        enc_grad_kernel, (array((width, feats)), array((1, feats), F32)),
        2 * tokens * feats * width, 1200000, own_inputs, pre_grad,
    )
    dec_grad = call(
        dec_grad_kernel, array(dec.shape), 5 * 2 * tokens * span * width, 3000000,
        source, error, codes,
    )
    return (recon_rows.astype(BF), enc_grad.T, bias_grad[0], dec_grad.T)


def solution(mesh):
    fine = Mesh(mesh.devices.reshape(LAYERS, 2, 2, 2, 4, 2, 2), AXES)
    wide = P(BLK, FEAT)
    in_specs = (wide, wide, wide, P(BLK), P(BLK, None), wide, P(BLK))
    out_specs = (wide, wide, P(BLK), wide)
    return jax.shard_map(body, mesh=fine, in_specs=in_specs, out_specs=out_specs, check_vma=False)
```

```python
import jax
import jax.numpy as jnp
from jax import lax
from jax.experimental import pallas as pl
from jax.experimental.pallas import tpu as pltpu
from jax.sharding import Mesh, PartitionSpec as P

LAYERS = 4
BF = jnp.bfloat16
F32 = jnp.float32
AXES = ("zh", "zm", "zb", "xh", "y", "xl", "core")
NEAR = ("zb", "xh", "y")
FEAT = ("xl", "core")
BLK = ("zh", "zm", "zb", "xh", "y")
VMEM_BYTES = 16 * 1024 * 1024


def exchange(pieces, axes):
    return lax.all_to_all(pieces, axes, 0, 0, tiled=True)


def share(piece, axes):
    count = lax.axis_size(axes)
    return exchange(jnp.broadcast_to(piece[None], (count,) + piece.shape), axes)


MIRRORED = [[0, 3], [1, 2]]
ADJACENT = [[0, 1], [2, 3]]


def both_of(piece, pairs):
    layer = lax.axis_index("zh")
    second = sum((layer == pair[1]).astype(jnp.int32) for pair in pairs)
    return lax.all_gather(piece, "zh", axis=0, axis_index_groups=pairs), 1 - second


def pick(pair, place):
    return jnp.where(place == 0, pair[0], pair[1])


def array(shape, dtype=BF):
    return jax.ShapeDtypeStruct(shape, dtype)


def own_slot(source, target):
    return pl.multiple_of(jnp.maximum(target - source, 0) * 256, 256)


def recon_kernel(source_ref, codes_ref, dec_ref, out_ref):
    source = source_ref[0]
    groups, _, rows, width = out_ref.shape
    span = codes_ref.shape[1] // 2
    for target in range(LAYERS):
        own = jnp.where(target >= source, codes_ref[:, :span], 0)
        other = jnp.where(target >= LAYERS - 1 - source, codes_ref[:, span:], 0)
        own_dec = dec_ref[:, pl.ds(own_slot(source, target), span)]
        other_dec = dec_ref[:, (target + 1) * span : (target + 2) * span]
        dims = (((1,), (1,)), ((), ()))
        total = lax.dot_general(own.astype(BF), own_dec, dims, preferred_element_type=F32)
        total += lax.dot_general(other.astype(BF), other_dec, dims, preferred_element_type=F32)
        out_ref[:, target] = total.astype(BF).reshape(groups, rows, width)


def terms_kernel(source_ref, error_ref, dec_ref, out_ref):
    source = source_ref[0]
    width = error_ref.shape[3]
    tokens, both = out_ref.shape
    span = both // 2
    own_sum = jnp.zeros((tokens, span), F32)
    other_sum = jnp.zeros((tokens, span), F32)
    for target in range(LAYERS):
        error = error_ref[:, target].reshape(tokens, width)
        own_dec = dec_ref[:, pl.ds(own_slot(source, target), span)]
        other_dec = dec_ref[:, (target + 1) * span : (target + 2) * span]
        own = jnp.dot(error, own_dec, preferred_element_type=F32)
        other = jnp.dot(error, other_dec, preferred_element_type=F32)
        own_sum += jnp.where(target >= source, own, 0.0)
        other_sum += jnp.where(target >= LAYERS - 1 - source, other, 0.0)
    out_ref[:, :span] = own_sum.astype(BF)
    out_ref[:, span:] = other_sum.astype(BF)


def dec_grad_kernel(source_ref, error_ref, codes_ref, out_ref):
    source = source_ref[0]
    width = error_ref.shape[3]
    tokens, both = codes_ref.shape
    span = both // 2
    for slot in range(LAYERS + 1):
        is_own = slot < LAYERS - source
        target = jnp.where(is_own, source + slot, slot - 1)
        error = error_ref[:, pl.ds(target, 1)].reshape(tokens, width)
        codes = jnp.where(is_own, codes_ref[:, :span], codes_ref[:, span:])
        grad = lax.dot_general(
            error, codes, (((0,), (0,)), ((), ())), preferred_element_type=F32
        )
        out_ref[:, slot * span : (slot + 1) * span] = grad.astype(BF)


def pre_kernel(inputs_ref, weight_ref, out_ref):
    pre = jnp.dot(inputs_ref[...], weight_ref[...], preferred_element_type=F32)
    out_ref[...] = pre.astype(BF)


def sum_kernel(pieces_ref, out_ref):
    for target in range(LAYERS):
        out_ref[target] = jnp.sum(pieces_ref[:, target].astype(F32), axis=0)


def enc_grad_kernel(inputs_ref, grad_ref, out_ref, bias_ref):
    grad = grad_ref[...]
    total = lax.dot_general(
        inputs_ref[...], grad, (((0,), (0,)), ((), ())), preferred_element_type=F32
    )
    out_ref[...] = total.astype(BF)
    bias_ref[...] = jnp.sum(grad.astype(F32), axis=0, keepdims=True)


def call(kernel, shapes, flops, moved, *operands):
    where = [pltpu.SMEM if operand.dtype == jnp.int32 else pltpu.VMEM for operand in operands]
    outs = jax.tree.map(lambda _: pl.BlockSpec(memory_space=pltpu.VMEM), shapes)
    return pl.pallas_call(
        kernel,
        out_shape=shapes,
        in_specs=[pl.BlockSpec(memory_space=space) for space in where],
        out_specs=outs,
        compiler_params=pltpu.CompilerParams(vmem_limit_bytes=VMEM_BYTES),
        cost_estimate=pl.CostEstimate(flops=flops, bytes_accessed=moved, transcendentals=0),
    )(*operands)


def body(layer_inputs, mlp_targets, enc_weight, enc_bias, act_mask, dec_weight, owner_half):
    source = lax.axis_index("zh").astype(jnp.int32).reshape(1)
    first = owner_half[0] == 0
    rows, width = layer_inputs.shape
    feats, tokens = act_mask.shape
    span = feats // 2
    parts = lax.axis_size(FEAT)
    near = lax.axis_size(NEAR)
    zm = lax.axis_size("zm")
    quarter = tokens // parts

    place = lax.axis_index(FEAT) * quarter + jnp.arange(quarter)
    token = place // rows % zm * (near * rows) + place // (rows * zm) * rows + place % rows
    picked = (token[:, None] == jnp.arange(tokens)[None, :]).astype(BF)
    mask_q = jnp.einsum("qm,fm->qf", picked, act_mask.astype(BF), preferred_element_type=F32)
    dec = dec_weight.T

    own_inputs = share(layer_inputs, NEAR + ("zm",)).reshape(tokens, width)
    pre_part = call(
        pre_kernel, array((tokens, feats)), 2 * tokens * feats * width, 1200000,
        own_inputs, enc_weight.T,
    ).reshape(parts, quarter, feats)
    pre = jnp.sum(exchange(pre_part, FEAT).astype(F32), axis=0) + enc_bias[None, :]
    code_q = (mask_q * pre).astype(BF)
    low, high = code_q[:, :span], code_q[:, span:]
    received = pick(*both_of(jnp.where(first, high, low), MIRRORED))
    both_q = jnp.concatenate([jnp.where(first, low, high), received], axis=1)
    codes = lax.all_gather(both_q, FEAT, axis=0, tiled=True)

    pieces = call(
        recon_kernel, array((near, LAYERS, zm * rows, width)), 8 * 2 * tokens * span * width, 3000000,
        source, codes, dec,
    )
    block = (LAYERS, zm, rows, width)
    sums = call(
        sum_kernel, array((LAYERS, zm * rows, width), F32), tokens * LAYERS * width, 1400000,
        exchange(pieces, NEAR),
    ).reshape(block)
    sums, targets = lax.optimization_barrier((sums, mlp_targets))
    layer, place = lax.axis_index("zh"), lax.axis_index("zm")
    mine = jnp.arange(LAYERS)[:, None] == layer
    mine = (mine & (jnp.arange(zm)[None, :] == place))[:, :, None, None]
    part = (sums - jnp.where(mine, targets.astype(F32)[None, None], 0.0)).astype(BF)

    def own_rows(array):
        return lax.dynamic_slice(array, (layer, place, 0, 0), (1, 1, rows, width))[0, 0]

    near_pair = lax.all_gather(part.reshape(LAYERS, zm * rows, width), "zm", axis=0)
    arrived = [(near_pair, 1 - place)]
    part = jnp.sum(near_pair.astype(F32), axis=0).astype(BF)
    for pairs in (MIRRORED, ADJACENT):
        pair, other = both_of(part, pairs)
        arrived.append((pair, other))
        part = jnp.sum(pair.astype(F32), axis=0).astype(BF)
    error = part
    error = share(error, NEAR).reshape(near, LAYERS, zm * rows, width)

    terms = call(
        terms_kernel, array((tokens, feats)), 8 * 2 * tokens * span * width, 3000000,
        source, error, dec,
    )
    terms, sums, arrived = lax.optimization_barrier((terms, sums, arrived))
    terms = exchange(terms.reshape(parts, quarter, feats), FEAT)
    terms_q = jnp.sum(terms.astype(F32), axis=0)
    recon_rows = own_rows(sums)
    for pair, other in arrived:
        recon_rows += own_rows(pick(pair, other).reshape(block)).astype(F32)
    returned = pick(*both_of(terms_q[:, span:].astype(BF), MIRRORED)).astype(F32)
    own = terms_q[:, :span]
    grad_q = jnp.concatenate(
        [jnp.where(first, own, returned), jnp.where(first, returned, own)], axis=1
    )
    pre_grad = lax.all_gather((mask_q * grad_q).astype(BF), FEAT, axis=0, tiled=True)
    enc_grad, bias_grad = call(
        enc_grad_kernel, (array((width, feats)), array((1, feats), F32)),
        2 * tokens * feats * width, 1200000, own_inputs, pre_grad,
    )
    dec_grad = call(
        dec_grad_kernel, array(dec.shape), 5 * 2 * tokens * span * width, 3000000,
        source, error, codes,
    )
    return (recon_rows.astype(BF), enc_grad.T, bias_grad[0], dec_grad.T)


def solution(mesh):
    fine = Mesh(mesh.devices.reshape(LAYERS, 2, 2, 2, 4, 2, 2), AXES)
    wide = P(BLK, FEAT)
    in_specs = (wide, wide, wide, P(BLK), P(BLK, None), wide, P(BLK))
    out_specs = (wide, wide, P(BLK), wide)
    return jax.shard_map(body, mesh=fine, in_specs=in_specs, out_specs=out_specs, check_vma=False)
```
